512 devices in a mesh: gx: 32 (over z, y_hi), gy: 16 (over x, y_lo, core).
Axes of the slice: x: 4, y: 8 (y_hi: 4, y_lo: 2; y = y_hi * 2 + y_lo), z: 8, core: 2. Of those that a mesh axis runs over, the one named last changes fastest.
Arguments:
- transfer: bfloat16 [32, 16, 2, 1024, 1024], P('gx', 'gy'), may hold values from -0.09375 to 0.09375
- sources: bfloat16 [32, 16, 2, 64, 1024], P('gx', 'gy'), may hold values from -6 to 6
- quad_nodes: int32 [8], replicated, may hold values from 0 to 7, each once
Outputs:
- outgoing: bfloat16 [32, 16, 2, 64, 1024], P('gx', 'gy')
The draws below stay inside these ranges and needn't reach their ends.
Inputs may be any that keep to these rules, and one draw needn't show every extreme that they name: `quad_nodes`: each node is used by exactly one block.
All inputs are finite; a program needn't handle non-finite values.
Results may differ from the reference program's by a relative error of at most 0.017.
Values may be sent and summed in bfloat16 or wider, within the bound.
A program may use at most 64 MiB of HBM per device.

```python
import math
import jax
import jax.numpy as jnp
from jax import lax

TRACE_ORDER = 1024
EDGE_CELLS = 512
RHS_DEV = 64
SPANS = 8
SECTIONS = 8
N_GX = 32
N_GY = 16


def block_levels(own_key, extent, pieces, least, largest):
    gain = 1.0
    for dim, shards_of in pieces:
        steps = jax.random.uniform(jax.random.fold_in(jax.random.fold_in(own_key, 6), dim), (shards_of,), jnp.float32, least / len(pieces), largest / len(pieces))
        gain = gain * jnp.repeat(jnp.exp(steps), extent[dim] // shards_of).reshape((-1,) + (1,) * (len(extent) - 1 - dim))
    return gain


def centred(key, extent, deviation, bound, shards=(), dtype=jnp.bfloat16):
    values = jax.random.normal(key, extent, jnp.float32) * deviation
    if len(shards) > 0:
        values = block_levels(key, extent, shards, -0.22, 0.18) * values
    return jnp.clip(values, min=-bound, max=bound).astype(dtype)


def setup_inputs(seed: int = 0) -> dict:
    key_list = jax.random.split(jax.random.key(seed), 4)
    return {
        "transfer": centred(key_list[0], (N_GX, N_GY, 2, TRACE_ORDER, TRACE_ORDER), (4 * TRACE_ORDER) ** -0.5, 0.09375, ((0, 32), (1, 16))),
        "sources": centred(key_list[1], (N_GX, N_GY, 2, RHS_DEV, TRACE_ORDER), 1.0, 6.0, ((0, 32), (1, 16))),
        "quad_nodes": jax.random.permutation(key_list[2], SPANS).astype(jnp.int32),
    }


def shift_columns(quad_nodes):
    angles = math.pi * (quad_nodes.astype(jnp.float32) + 0.5) / SPANS
    sig_re = jnp.repeat(0.5 * jnp.cos(angles), RHS_DEV // SPANS)[:, None]
    sig_im = jnp.repeat(0.5 * jnp.sin(angles), RHS_DEV // SPANS)[:, None]
    return sig_re, sig_im


def reference(transfer, sources, quad_nodes):
    sig_re, sig_im = shift_columns(quad_nodes)
    shape = sources.shape
    incoming = jnp.zeros(shape, jnp.bfloat16)
    flat_w = transfer.reshape(-1, 2, TRACE_ORDER, TRACE_ORDER)

    def apply_block(pair):
        driven, weights = pair
        u_re, u_im = driven[0], driven[1]
        real_part = jnp.dot(u_re, weights[0], preferred_element_type=jnp.float32) - jnp.dot(u_im, weights[1], preferred_element_type=jnp.float32)
        imag_part = jnp.dot(u_re, weights[1], preferred_element_type=jnp.float32) + jnp.dot(u_im, weights[0], preferred_element_type=jnp.float32)
        f_re = u_re.astype(jnp.float32)
        f_im = u_im.astype(jnp.float32)
        real_part = real_part + sig_re * f_re - sig_im * f_im
        imag_part = imag_part + sig_re * f_im + sig_im * f_re
        return jnp.stack([real_part, imag_part]).astype(jnp.bfloat16)

    outgoing = incoming
    for section_index in range(SECTIONS):
        driven = (incoming.astype(jnp.float32) + sources.astype(jnp.float32)).astype(jnp.bfloat16)
        outgoing = lax.map(apply_block, (driven.reshape(-1, 2, RHS_DEV, TRACE_ORDER), flat_w)).reshape(shape)
        if section_index + 1 < SECTIONS:
            right_side = outgoing[..., :EDGE_CELLS]
            top_side = outgoing[..., EDGE_CELLS:]
            in_left = jnp.concatenate([jnp.zeros_like(right_side[:1]), right_side[:-1]], axis=0)
            in_bottom = jnp.concatenate([jnp.zeros_like(top_side[:, :1]), top_side[:, :-1]], axis=1)
            incoming = jnp.concatenate([in_left, in_bottom], axis=-1)
    return outgoing
```

```python
import functools
import math

import jax
import jax.numpy as jnp
from jax import lax
from jax.experimental import pallas as pl
from jax.experimental.pallas import tpu as pltpu
from jax.sharding import PartitionSpec as P

SPANS = 8
SECTIONS = 8
CHUNKS = 2
PIECES = 4
MESH = pl.DeviceIdType.MESH


def kernel(
    n_gx, n_gy, nodes_ref, w_hbm, src_hbm, out_hbm,
    w, src, in_left, in_bottom, out_right, out_top, sig_re, sig_im,
    w_sem, src_sem, out_sem, send_right, recv_left, send_top, recv_bottom,
):
    gx, gy = lax.axis_index("gx"), lax.axis_index("gy")
    rows, order = src.shape[1], src.shape[2]
    edge = order // 2
    step = rows // CHUNKS
    depth = order // PIECES
    has_left, has_bottom = gx > 0, gy > 0
    has_right, has_top = gx < n_gx - 1, gy < n_gy - 1

    load_src = pltpu.make_async_copy(src_hbm, src, src_sem)
    load_src.start()

    def load_w(half, piece):
        part = (slice(None), pl.ds(piece * depth, depth), pl.ds(half * edge, edge))
        return pltpu.make_async_copy(w_hbm.at[part], w.at[part], w_sem.at[half, piece])

    for half in range(2):
        for piece in range(PIECES):
            load_w(half, piece).start()

    barrier = pltpu.get_barrier_semaphore()
    neighbours = (
        (has_left, (gx - 1, gy)), (has_right, (gx + 1, gy)),
        (has_bottom, (gx, gy - 1)), (has_top, (gx, gy + 1)),
    )
    for there, device in neighbours:
        @pl.when(there)
        def _():
            pl.semaphore_signal(barrier, inc=1, device_id=device, device_id_type=MESH)

    @pl.when(jnp.logical_not(has_left))
    def _():
        in_left[...] = jnp.zeros_like(in_left)

    @pl.when(jnp.logical_not(has_bottom))
    def _():
        in_bottom[...] = jnp.zeros_like(in_bottom)

    block = rows // SPANS
    nodes = jnp.concatenate(
        [jnp.full((block, 128), nodes_ref[b].astype(jnp.float32)) for b in range(SPANS)], axis=0
    )
    angles = math.pi * (nodes + 0.5) / SPANS
    sig_re[...] = 0.5 * jnp.cos(angles)
    sig_im[...] = 0.5 * jnp.sin(angles)

    def send(side, section, chunk):
        if side == 0:
            return pltpu.make_async_remote_copy(
                src_ref=out_right.at[section, chunk], dst_ref=in_left.at[section, chunk],
                send_sem=send_right.at[section, chunk], recv_sem=recv_left.at[section, chunk],
                device_id=(gx + 1, gy), device_id_type=MESH,
            )
        return pltpu.make_async_remote_copy(
            src_ref=out_top.at[section, chunk], dst_ref=in_bottom.at[section, chunk],
            send_sem=send_top.at[section, chunk], recv_sem=recv_bottom.at[section, chunk],
            device_id=(gx, gy + 1), device_id_type=MESH,
        )

    def finish(side, section, chunk, driven, real, imag):
        span = pl.ds(chunk * step, step)
        f = driven[:, side * edge:(side + 1) * edge].astype(jnp.float32)
        f_re, f_im = f[:step], f[step:]
        s_re = jnp.concatenate([sig_re[span, :]] * (edge // 128), axis=1)
        s_im = jnp.concatenate([sig_im[span, :]] * (edge // 128), axis=1)
        out = out_right if side == 0 else out_top
        out[section, chunk, 0] = (real + s_re * f_re - s_im * f_im).astype(jnp.bfloat16)
        out[section, chunk, 1] = (imag + s_re * f_im + s_im * f_re).astype(jnp.bfloat16)

    def product(driven, side, first, size):
        u = driven[:, first:first + size]
        columns = slice(side * edge, (side + 1) * edge)
        p = jnp.dot(u, w[0, first:first + size, columns], preferred_element_type=jnp.float32)
        q = jnp.dot(u, w[1, first:first + size, columns], preferred_element_type=jnp.float32)
        return p[:step] - q[step:], q[:step] + p[step:]

    def source(chunk):
        span = pl.ds(chunk * step, step)
        return jnp.concatenate([src[0, span, :], src[1, span, :]], axis=0)

    load_src.wait()
    for side in range(2):
        totals = [[0.0, 0.0] for _ in range(CHUNKS)]
        for piece in range(PIECES):
            load_w(side, piece).wait()
            for chunk in range(CHUNKS):
                real, imag = product(source(chunk), side, piece * depth, depth)
                totals[chunk][0] += real
                totals[chunk][1] += imag
        for chunk in range(CHUNKS):
            finish(side, 0, chunk, source(chunk), *totals[chunk])
            if side == 0 and chunk == 0:
                pl.semaphore_wait(
                    barrier,
                    has_left.astype(jnp.int32) + has_right.astype(jnp.int32)
                    + has_bottom.astype(jnp.int32) + has_top.astype(jnp.int32),
                )

            @pl.when(has_right if side == 0 else has_top)
            def _():
                send(side, 0, chunk).start()

    def section_body(section, _):
        for chunk in range(CHUNKS):
            @pl.when(has_bottom)
            def _():
                send(1, section - 1, chunk).wait_recv()

            @pl.when(has_left)
            def _():
                send(0, section - 1, chunk).wait_recv()

            span = pl.ds(chunk * step, step)
            driven = jnp.concatenate(
                [
                    jnp.concatenate(
                        [
                            in_left[section - 1, chunk, part].astype(jnp.float32),
                            in_bottom[section - 1, chunk, part].astype(jnp.float32),
                        ],
                        axis=1,
                    )
                    + src[part, span, :].astype(jnp.float32)
                    for part in range(2)
                ],
                axis=0,
            ).astype(jnp.bfloat16)
            for side in range(2):
                real, imag = product(driven, side, 0, order)
                finish(side, section, chunk, driven, real, imag)

                @pl.when(jnp.logical_and(has_right if side == 0 else has_top, section < SECTIONS - 1))
                def _():
                    send(side, section, chunk).start()
        return 0

    lax.fori_loop(1, SECTIONS, section_body, 0)

    def store(side, chunk):
        out = out_right if side == 0 else out_top
        return pltpu.make_async_copy(
            out.at[SECTIONS - 1, chunk],
            out_hbm.at[:, pl.ds(chunk * step, step), pl.ds(side * edge, edge)],
            out_sem.at[side, chunk],
        )

    for chunk in range(CHUNKS):
        for side in range(2):
            store(side, chunk).start()

    def drain(section, _):
        for chunk in range(CHUNKS):
            @pl.when(has_right)
            def _():
                send(0, section, chunk).wait_send()

            @pl.when(has_top)
            def _():
                send(1, section, chunk).wait_send()
        return 0

    lax.fori_loop(0, SECTIONS - 1, drain, 0)
    for chunk in range(CHUNKS):
        for side in range(2):
            store(side, chunk).wait()


def solution(mesh):
    n_gx, n_gy = mesh.shape["gx"], mesh.shape["gy"]

    def per_device(transfer, sources, quad_nodes):
        weights, source = transfer[0, 0], sources[0, 0]
        _, rows, order = source.shape
        step, edge = rows // CHUNKS, order // 2
        moved = SECTIONS - 1
        dma = pltpu.SemaphoreType.DMA
        outgoing = pl.pallas_call(
            functools.partial(kernel, n_gx, n_gy),
            out_shape=jax.ShapeDtypeStruct(source.shape, jnp.bfloat16),
            in_specs=[
                pl.BlockSpec(memory_space=pltpu.SMEM),
                pl.BlockSpec(memory_space=pl.ANY),
                pl.BlockSpec(memory_space=pl.ANY),
            ],
            out_specs=pl.BlockSpec(memory_space=pl.ANY),
            scratch_shapes=[
                pltpu.VMEM(weights.shape, jnp.bfloat16),
                pltpu.VMEM(source.shape, jnp.bfloat16),
                pltpu.VMEM((moved, CHUNKS, 2, step, edge), jnp.bfloat16),
                pltpu.VMEM((moved, CHUNKS, 2, step, edge), jnp.bfloat16),
                pltpu.VMEM((SECTIONS, CHUNKS, 2, step, edge), jnp.bfloat16),
                pltpu.VMEM((SECTIONS, CHUNKS, 2, step, edge), jnp.bfloat16),
                pltpu.VMEM((rows, 128), jnp.float32),
                pltpu.VMEM((rows, 128), jnp.float32),
                dma((2, PIECES)),
                dma,
                dma((2, CHUNKS)),
                dma((moved, CHUNKS)),
                dma((moved, CHUNKS)),
                dma((moved, CHUNKS)),
                dma((moved, CHUNKS)),
            ],
            compiler_params=pltpu.CompilerParams(
                collective_id=0, has_side_effects=True, vmem_limit_bytes=60 * 1024 * 1024
            ),
        )(quad_nodes, weights, source)
        return outgoing[None, None]

    return jax.shard_map(
        per_device,
        mesh=mesh,
        in_specs=(P("gx", "gy", None, None, None), P("gx", "gy", None, None, None), P()),
        out_specs=P("gx", "gy", None, None, None),
        check_vma=False,
    )
```

```python
import functools
import math

import jax
import jax.numpy as jnp
from jax import lax
from jax.experimental import pallas as pl
from jax.experimental.pallas import tpu as pltpu
from jax.sharding import PartitionSpec as P

SPANS = 8
SECTIONS = 8
GROUPS = 4
PIECES = 4
PERIOD = 2
RELAY_SLOT = (4, 0)
FIRST_SLOT = (0, 2)
Y_HI, Y_LO, CORES = 4, 2, 2
RING = Y_HI * Y_LO
BACK = 3
MESH = pl.DeviceIdType.MESH


def kernel(
    n_gx, n_gy, nodes_ref, w_hbm, src_hbm, out_hbm,
    w, src, in_left, in_bottom, out_right, out_top, relay, sig_re, sig_im,
    w_sem, src_sem, out_sem, send_right, recv_left, send_top, recv_bottom, recv_relay, send_relay,
):
    gx, gy = lax.axis_index("gx"), lax.axis_index("gy")
    step, order = src.shape[2], src.shape[3]
    edge = order // 2
    depth = order // PIECES
    has_left, has_bottom = gx > 0, gy > 0
    has_right, has_top = gx < n_gx - 1, gy < n_gy - 1

    z, y = gx // Y_HI, (gx % Y_HI) * Y_LO + (gy // CORES) % Y_LO

    def on_ring(level, place):
        column = level * Y_HI + place // Y_LO
        row = (gy // (Y_LO * CORES)) * (Y_LO * CORES) + (place % Y_LO) * CORES + gy % CORES
        return column, row

    behind, ahead = (y + RING - BACK) % RING, (y + BACK) % RING
    relay_to = on_ring(z, behind)
    relay_from = on_ring(z, ahead)
    has_relay = relay_from[0] < n_gx - 1
    last_to = on_ring(z + (ahead // Y_LO + 1) // Y_HI, behind)
    origin = gx - 1
    last_from = on_ring(origin // Y_HI, ((origin % Y_HI) * Y_LO + (gy // CORES) % Y_LO + RING - BACK) % RING)

    def load_src(group):
        return pltpu.make_async_copy(
            src_hbm.at[:, pl.ds(group * step, step), :], src.at[group], src_sem.at[group]
        )

    def load_w(half, piece):
        part = (slice(None), pl.ds(piece * depth, depth), pl.ds(half * edge, edge))
        return pltpu.make_async_copy(w_hbm.at[part], w.at[part], w_sem.at[half, piece])

    barrier = pltpu.get_barrier_semaphore()
    for there, device in (
        (has_left, (gx - 1, gy)), (has_bottom, (gx, gy - 1)),
        (has_relay, relay_from), (has_left, last_from),
    ):
        @pl.when(there)
        def _():
            pl.semaphore_signal(barrier, inc=1, device_id=device, device_id_type=MESH)

    for group in range(GROUPS):
        load_src(group).start()
    for half in range(2):
        for piece in range(PIECES):
            load_w(half, piece).start()

    @pl.when(jnp.logical_not(has_left))
    def _():
        in_left[...] = jnp.zeros_like(in_left)

    @pl.when(jnp.logical_not(has_bottom))
    def _():
        in_bottom[...] = jnp.zeros_like(in_bottom)

    block = GROUPS * step // SPANS
    nodes = jnp.concatenate(
        [jnp.full((block, 128), nodes_ref[b].astype(jnp.float32)) for b in range(SPANS)], axis=0
    )
    angles = math.pi * (nodes + 0.5) / SPANS
    sig_re[...] = (0.5 * jnp.cos(angles)).reshape(sig_re.shape)
    sig_im[...] = (0.5 * jnp.sin(angles)).reshape(sig_im.shape)

    def copy_out(out, section, group, dst, send_sem, recv_sem, device):
        return pltpu.make_async_remote_copy(
            src_ref=out.at[section, group], dst_ref=dst,
            send_sem=send_sem.at[section, group], recv_sem=recv_sem,
            device_id=device, device_id_type=MESH,
        )

    def direct(section, group):
        return copy_out(
            out_right, section, group, in_left.at[section, group],
            send_right, recv_left.at[section, group], (gx + 1, gy),
        )

    def first_leg(section, group):
        return copy_out(
            out_right, section, group, relay.at[section],
            send_right, recv_relay.at[section], relay_to,
        )

    def last_leg(section, group):
        return pltpu.make_async_remote_copy(
            src_ref=relay.at[section], dst_ref=in_left.at[section, group],
            send_sem=send_relay.at[section], recv_sem=recv_left.at[section, group],
            device_id=last_to, device_id_type=MESH,
        )

    def upward(section, group):
        return copy_out(
            out_top, section, group, in_bottom.at[section, group],
            send_top, recv_bottom.at[section, group], (gx, gy + 1),
        )

    def turned(section):
        return section % PERIOD == 0

    def first_group(section):
        return (section + PERIOD - 1) // PERIOD % GROUPS

    def send(side, place, section, group):
        if side == 1:
            upward(section, group).start()
        elif place > 0:
            direct(section, group).start()
        else:
            @pl.when(turned(section))
            def _():
                first_leg(section, group).start()

            @pl.when(jnp.logical_not(turned(section)))
            def _():
                direct(section, group).start()

    def pass_on(section, when):
        @pl.when(jnp.logical_and(has_relay, jnp.logical_and(when, turned(section))))
        def _():
            first_leg(section, 0).wait_recv()
            last_leg(section, first_group(section)).start()

    def product(u, side, first, size):
        half = u.shape[0] // 2
        columns = slice(side * edge, (side + 1) * edge)
        p = jnp.dot(u, w[0, first:first + size, columns], preferred_element_type=jnp.float32)
        q = jnp.dot(u, w[1, first:first + size, columns], preferred_element_type=jnp.float32)
        return p[:half] - q[half:], q[:half] + p[half:]

    def finish(side, section, group, f_re, f_im, real, imag):
        s_re = jnp.concatenate([sig_re[group]] * (edge // 128), axis=1)
        s_im = jnp.concatenate([sig_im[group]] * (edge // 128), axis=1)
        out = out_right if side == 0 else out_top
        out[section, group, 0] = (real + s_re * f_re - s_im * f_im).astype(jnp.bfloat16)
        out[section, group, 1] = (imag + s_re * f_im + s_im * f_re).astype(jnp.bfloat16)

    for group in range(GROUPS):
        load_src(group).wait()
    for side in range(2):
        real, imag = 0.0, 0.0
        columns = slice(side * edge, (side + 1) * edge)
        for piece in range(PIECES):
            load_w(side, piece).wait()
            part = slice(piece * depth, (piece + 1) * depth)
            u = jnp.concatenate(
                [src[group, c, :, part] for c in range(2) for group in range(GROUPS)], axis=0
            )
            more_real, more_imag = product(u, side, 0 + piece * depth, depth)
            real += more_real
            imag += more_imag
        for group in range(GROUPS):
            rows = slice(group * step, (group + 1) * step)
            finish(
                side, 0, group,
                src[group, 0, :, columns].astype(jnp.float32),
                src[group, 1, :, columns].astype(jnp.float32),
                real[rows], imag[rows],
            )
        if side == 0:
            pl.semaphore_wait(
                barrier, 2 * has_right.astype(jnp.int32) + has_top.astype(jnp.int32) + has_relay.astype(jnp.int32)
            )
        for group in range(GROUPS):
            @pl.when(has_right if side == 0 else has_top)
            def _():
                send(side, group, jnp.int32(0), group)

    def section_body(section, _):
        more = section < SECTIONS - 1

        def relay_slot(place, phase):
            if (place, phase) == FIRST_SLOT:
                pass_on(section - 1, section == 1)
            if (place, phase) == RELAY_SLOT:
                pass_on(section, more)
            if (place + GROUPS, phase) == RELAY_SLOT and place + phase > 0:
                pass_on(section - 1, section > 1)

        for place in range(GROUPS):
            group = (first_group(section) + place) % GROUPS
            relay_slot(place, 0)

            def arrived(buffer, columns):
                return [
                    (
                        buffer[section - 1, group, part].astype(jnp.float32)
                        + src[group, part, :, columns].astype(jnp.float32)
                    ).astype(jnp.bfloat16)
                    for part in range(2)
                ]

            @pl.when(has_bottom)
            def _():
                upward(section - 1, group).wait_recv()

            lower = arrived(in_bottom, slice(edge, order))
            u = jnp.concatenate(lower, axis=0)
            partial = [product(u, side, edge, edge) for side in range(2)]
            relay_slot(place, 1)

            @pl.when(has_left)
            def _():
                direct(section - 1, group).wait_recv()

            upper = arrived(in_left, slice(0, edge))
            u = jnp.concatenate(upper, axis=0)
            for side, driven in ((0, upper), (1, lower)):
                real, imag = product(u, side, 0, edge)
                finish(
                    side, section, group,
                    driven[0].astype(jnp.float32), driven[1].astype(jnp.float32),
                    partial[side][0] + real, partial[side][1] + imag,
                )

                @pl.when(jnp.logical_and(has_right if side == 0 else has_top, more))
                def _():
                    send(side, place, section, group)

                if side == 0:
                    relay_slot(place, 2)
        relay_slot(GROUPS, 0)
        return 0

    lax.fori_loop(1, SECTIONS, section_body, 0)

    def store(side, group):
        out = out_right if side == 0 else out_top
        return pltpu.make_async_copy(
            out.at[SECTIONS - 1, group],
            out_hbm.at[:, pl.ds(group * step, step), pl.ds(side * edge, edge)],
            out_sem.at[side, group],
        )

    for group in range(GROUPS):
        for side in range(2):
            store(side, group).start()

    def drain(section, _):
        for group in range(GROUPS):
            @pl.when(has_right)
            def _():
                direct(section, group).wait_send()

            @pl.when(has_top)
            def _():
                upward(section, group).wait_send()

        @pl.when(jnp.logical_and(has_relay, turned(section)))
        def _():
            last_leg(section, 0).wait_send()
        return 0

    lax.fori_loop(0, SECTIONS - 1, drain, 0)
    for group in range(GROUPS):
        for side in range(2):
            store(side, group).wait()


def solution(mesh):
    n_gx, n_gy = mesh.shape["gx"], mesh.shape["gy"]

    def per_device(transfer, sources, quad_nodes):
        weights, source = transfer[0, 0], sources[0, 0]
        _, rows, order = source.shape
        step, edge = rows // GROUPS, order // 2
        moved = SECTIONS - 1
        dma = pltpu.SemaphoreType.DMA
        vmem = pltpu.VMEM
        outgoing = pl.pallas_call(
            functools.partial(kernel, n_gx, n_gy),
            out_shape=jax.ShapeDtypeStruct(source.shape, jnp.bfloat16),
            in_specs=[
                pl.BlockSpec(memory_space=pltpu.SMEM),
                pl.BlockSpec(memory_space=pl.ANY),
                pl.BlockSpec(memory_space=pl.ANY),
            ],
            out_specs=pl.BlockSpec(memory_space=pl.ANY),
            scratch_shapes=[
                vmem(weights.shape, jnp.bfloat16),
                vmem((GROUPS, 2, step, order), jnp.bfloat16),
                vmem((moved, GROUPS, 2, step, edge), jnp.bfloat16),
                vmem((moved, GROUPS, 2, step, edge), jnp.bfloat16),
                vmem((SECTIONS, GROUPS, 2, step, edge), jnp.bfloat16),
                vmem((SECTIONS, GROUPS, 2, step, edge), jnp.bfloat16),
                vmem((moved, 2, step, edge), jnp.bfloat16),
                vmem((GROUPS, step, 128), jnp.float32),
                vmem((GROUPS, step, 128), jnp.float32),
                dma((2, PIECES)),
                dma((GROUPS,)),
                dma((2, GROUPS)),
                dma((moved, GROUPS)),
                dma((moved, GROUPS)),
                dma((moved, GROUPS)),
                dma((moved, GROUPS)),
                dma((moved,)),
                dma((moved,)),
            ],
            compiler_params=pltpu.CompilerParams(
                collective_id=0, has_side_effects=True, vmem_limit_bytes=60 * 1024 * 1024
            ),
        )(quad_nodes, weights, source)
        return outgoing[None, None]

    return jax.shard_map(
        per_device,
        mesh=mesh,
        in_specs=(P("gx", "gy", None, None, None), P("gx", "gy", None, None, None), P()),
        out_specs=P("gx", "gy", None, None, None),
        check_vma=False,
    )
```

```python
import functools
import math

import jax
import jax.numpy as jnp
from jax import lax
from jax.experimental import pallas as pl
from jax.experimental.pallas import tpu as pltpu
from jax.sharding import PartitionSpec as P

SPANS = 8
SECTIONS = 8
GROUPS = 4
PIECES = 4
PERIOD = 2
RELAY_SLOT = (4, 0)
FIRST_SLOT = (0, 2)
Y_HI, Y_LO, CORES = 4, 2, 2
RING = Y_HI * Y_LO
BACK = 3
MESH = pl.DeviceIdType.MESH


def kernel(
    n_gx, n_gy, nodes_ref, w_hbm, src_hbm, out_ref,
    w, src, in_left, in_bottom, out_right, out_top, relay, sig_re, sig_im,
    w_sem, src_sem, send_right, recv_left, send_top, recv_bottom, recv_relay, send_relay,
):
    gx, gy = lax.axis_index("gx"), lax.axis_index("gy")
    step, order = src.shape[2], src.shape[3]
    edge = order // 2
    depth = order // PIECES
    has_left, has_bottom = gx > 0, gy > 0
    has_right, has_top = gx < n_gx - 1, gy < n_gy - 1

    z, y = gx // Y_HI, (gx % Y_HI) * Y_LO + (gy // CORES) % Y_LO

    def on_ring(level, place):
        column = level * Y_HI + place // Y_LO
        row = (gy // (Y_LO * CORES)) * (Y_LO * CORES) + (place % Y_LO) * CORES + gy % CORES
        return column, row

    behind, ahead = (y + RING - BACK) % RING, (y + BACK) % RING
    relay_to = on_ring(z, behind)
    relay_from = on_ring(z, ahead)
    has_relay = relay_from[0] < n_gx - 1
    last_to = on_ring(z + (ahead // Y_LO + 1) // Y_HI, behind)
    origin = gx - 1
    last_from = on_ring(origin // Y_HI, ((origin % Y_HI) * Y_LO + (gy // CORES) % Y_LO + RING - BACK) % RING)

    def load_src(group):
        return pltpu.make_async_copy(
            src_hbm.at[:, pl.ds(group * step, step), :], src.at[group], src_sem.at[group]
        )

    def load_w(half, piece):
        part = (slice(None), pl.ds(piece * depth, depth), pl.ds(half * edge, edge))
        return pltpu.make_async_copy(w_hbm.at[part], w.at[part], w_sem.at[half, piece])

    barrier = pltpu.get_barrier_semaphore()
    for there, device in (
        (has_left, (gx - 1, gy)), (has_bottom, (gx, gy - 1)),
        (has_relay, relay_from), (has_left, last_from),
    ):
        @pl.when(there)
        def _():
            pl.semaphore_signal(barrier, inc=1, device_id=device, device_id_type=MESH)

    for group in range(GROUPS):
        load_src(group).start()
    for half in range(2):
        for piece in range(PIECES):
            load_w(half, piece).start()

    @pl.when(jnp.logical_not(has_left))
    def _():
        in_left[...] = jnp.zeros_like(in_left)

    @pl.when(jnp.logical_not(has_bottom))
    def _():
        in_bottom[...] = jnp.zeros_like(in_bottom)

    block = GROUPS * step // SPANS
    nodes = jnp.concatenate(
        [jnp.full((block, 128), nodes_ref[b].astype(jnp.float32)) for b in range(SPANS)], axis=0
    )
    angles = math.pi * (nodes + 0.5) / SPANS
    sig_re[...] = (0.5 * jnp.cos(angles)).reshape(sig_re.shape)
    sig_im[...] = (0.5 * jnp.sin(angles)).reshape(sig_im.shape)

    def copy_out(out, section, group, dst, send_sem, recv_sem, device):
        return pltpu.make_async_remote_copy(
            src_ref=out.at[section, group], dst_ref=dst,
            send_sem=send_sem.at[section, group], recv_sem=recv_sem,
            device_id=device, device_id_type=MESH,
        )

    def direct(section, group):
        return copy_out(
            out_right, section, group, in_left.at[section, group],
            send_right, recv_left.at[section, group], (gx + 1, gy),
        )

    def first_leg(section, group):
        return copy_out(
            out_right, section, group, relay.at[section],
            send_right, recv_relay.at[section], relay_to,
        )

    def last_leg(section, group):
        return pltpu.make_async_remote_copy(
            src_ref=relay.at[section], dst_ref=in_left.at[section, group],
            send_sem=send_relay.at[section], recv_sem=recv_left.at[section, group],
            device_id=last_to, device_id_type=MESH,
        )

    def upward(section, group):
        return copy_out(
            out_top, section, group, in_bottom.at[section, group],
            send_top, recv_bottom.at[section, group], (gx, gy + 1),
        )

    def turned(section):
        return section % PERIOD == 0

    def first_group(section):
        return (section + PERIOD - 1) // PERIOD % GROUPS

    def send(side, place, section, group):
        if side == 1:
            upward(section, group).start()
        elif place > 0:
            direct(section, group).start()
        else:
            @pl.when(turned(section))
            def _():
                first_leg(section, group).start()

            @pl.when(jnp.logical_not(turned(section)))
            def _():
                direct(section, group).start()

    def pass_on(section, when):
        @pl.when(jnp.logical_and(has_relay, jnp.logical_and(when, turned(section))))
        def _():
            first_leg(section, 0).wait_recv()
            last_leg(section, first_group(section)).start()

    def product(u, side, first, size):
        half = u.shape[0] // 2
        columns = slice(side * edge, (side + 1) * edge)
        p = jnp.dot(u, w[0, first:first + size, columns], preferred_element_type=jnp.float32)
        q = jnp.dot(u, w[1, first:first + size, columns], preferred_element_type=jnp.float32)
        return p[:half] - q[half:], q[:half] + p[half:]

    def finish(side, section, group, f_re, f_im, real, imag):
        s_re = jnp.concatenate([sig_re[group]] * (edge // 128), axis=1)
        s_im = jnp.concatenate([sig_im[group]] * (edge // 128), axis=1)
        out = out_right if side == 0 else out_top
        out[section, group, 0] = (real + s_re * f_re - s_im * f_im).astype(jnp.bfloat16)
        out[section, group, 1] = (imag + s_re * f_im + s_im * f_re).astype(jnp.bfloat16)

    for group in range(GROUPS):
        load_src(group).wait()
    for side in range(2):
        real, imag = 0.0, 0.0
        columns = slice(side * edge, (side + 1) * edge)
        for piece in range(PIECES):
            load_w(side, piece).wait()
            part = slice(piece * depth, (piece + 1) * depth)
            u = jnp.concatenate(
                [src[group, c, :, part] for c in range(2) for group in range(GROUPS)], axis=0
            )
            more_real, more_imag = product(u, side, 0 + piece * depth, depth)
            real += more_real
            imag += more_imag
        for group in range(GROUPS):
            rows = slice(group * step, (group + 1) * step)
            finish(
                side, 0, group,
                src[group, 0, :, columns].astype(jnp.float32),
                src[group, 1, :, columns].astype(jnp.float32),
                real[rows], imag[rows],
            )
        if side == 0:
            pl.semaphore_wait(
                barrier, 2 * has_right.astype(jnp.int32) + has_top.astype(jnp.int32) + has_relay.astype(jnp.int32)
            )
        for group in range(GROUPS):
            @pl.when(has_right if side == 0 else has_top)
            def _():
                send(side, group, jnp.int32(0), group)

    def section_body(section, _):
        more = section < SECTIONS - 1

        def relay_slot(place, phase):
            if (place, phase) == FIRST_SLOT:
                pass_on(section - 1, section == 1)
            if (place, phase) == RELAY_SLOT:
                pass_on(section, more)
            if (place + GROUPS, phase) == RELAY_SLOT and place + phase > 0:
                pass_on(section - 1, section > 1)

        for place in range(GROUPS):
            group = (first_group(section) + place) % GROUPS
            relay_slot(place, 0)

            def arrived(buffer, columns):
                return [
                    (
                        buffer[section - 1, group, part].astype(jnp.float32)
                        + src[group, part, :, columns].astype(jnp.float32)
                    ).astype(jnp.bfloat16)
                    for part in range(2)
                ]

            @pl.when(has_bottom)
            def _():
                upward(section - 1, group).wait_recv()

            lower = arrived(in_bottom, slice(edge, order))
            u = jnp.concatenate(lower, axis=0)
            partial = [product(u, side, edge, edge) for side in range(2)]
            relay_slot(place, 1)

            @pl.when(has_left)
            def _():
                direct(section - 1, group).wait_recv()

            upper = arrived(in_left, slice(0, edge))
            u = jnp.concatenate(upper, axis=0)
            for side, driven in ((0, upper), (1, lower)):
                real, imag = product(u, side, 0, edge)
                finish(
                    side, section, group,
                    driven[0].astype(jnp.float32), driven[1].astype(jnp.float32),
                    partial[side][0] + real, partial[side][1] + imag,
                )

                @pl.when(jnp.logical_and(has_right if side == 0 else has_top, more))
                def _():
                    send(side, place, section, group)

                if side == 0:
                    relay_slot(place, 2)
        relay_slot(GROUPS, 0)
        return 0

    lax.fori_loop(1, SECTIONS, section_body, 0)

    for group in range(GROUPS):
        rows = pl.ds(group * step, step)
        out_ref[:, rows, :edge] = out_right[SECTIONS - 1, group]
        out_ref[:, rows, edge:] = out_top[SECTIONS - 1, group]

    def drain(section, _):
        for group in range(GROUPS):
            @pl.when(has_right)
            def _():
                direct(section, group).wait_send()

            @pl.when(has_top)
            def _():
                upward(section, group).wait_send()

        @pl.when(jnp.logical_and(has_relay, turned(section)))
        def _():
            last_leg(section, 0).wait_send()
        return 0

    lax.fori_loop(0, SECTIONS - 1, drain, 0)


def solution(mesh):
    n_gx, n_gy = mesh.shape["gx"], mesh.shape["gy"]

    def per_device(transfer, sources, quad_nodes):
        weights, source = transfer[0, 0], sources[0, 0]
        _, rows, order = source.shape
        step, edge = rows // GROUPS, order // 2
        moved = SECTIONS - 1
        dma = pltpu.SemaphoreType.DMA
        vmem = pltpu.VMEM
        outgoing = pl.pallas_call(
            functools.partial(kernel, n_gx, n_gy),
            out_shape=pltpu.VMEM(source.shape, jnp.bfloat16),
            in_specs=[
                pl.BlockSpec(memory_space=pltpu.SMEM),
                pl.BlockSpec(memory_space=pl.ANY),
                pl.BlockSpec(memory_space=pl.ANY),
            ],
            out_specs=pl.BlockSpec(memory_space=pltpu.VMEM),
            scratch_shapes=[
                vmem(weights.shape, jnp.bfloat16),
                vmem((GROUPS, 2, step, order), jnp.bfloat16),
                vmem((moved, GROUPS, 2, step, edge), jnp.bfloat16),
                vmem((moved, GROUPS, 2, step, edge), jnp.bfloat16),
                vmem((SECTIONS, GROUPS, 2, step, edge), jnp.bfloat16),
                vmem((SECTIONS, GROUPS, 2, step, edge), jnp.bfloat16),
                vmem((moved, 2, step, edge), jnp.bfloat16),
                vmem((GROUPS, step, 128), jnp.float32),
                vmem((GROUPS, step, 128), jnp.float32),
                dma((2, PIECES)),
                dma((GROUPS,)),
                dma((moved, GROUPS)),
                dma((moved, GROUPS)),
                dma((moved, GROUPS)),
                dma((moved, GROUPS)),
                dma((moved,)),
                dma((moved,)),
            ],
            compiler_params=pltpu.CompilerParams(
                collective_id=0, has_side_effects=True, vmem_limit_bytes=60 * 1024 * 1024
            ),
        )(quad_nodes, weights, source)
        return outgoing[None, None]

    return jax.shard_map(
        per_device,
        mesh=mesh,
        in_specs=(P("gx", "gy", None, None, None), P("gx", "gy", None, None, None), P()),
        out_specs=P("gx", "gy", None, None, None),
        check_vma=False,
    )
```

```python
import functools
import math

import jax
import jax.numpy as jnp
from jax import lax
from jax.experimental import pallas as pl
from jax.experimental.pallas import tpu as pltpu
from jax.sharding import PartitionSpec as P

SPANS = 8
SECTIONS = 8
GROUPS = 4
PIECES = 4
TURNED = (0, 2, 4, 5)
RELAY_SLOT = (4, 0)
FIRST_SLOT = (0, 2)
Y_HI, Y_LO, CORES = 4, 2, 2
RING = Y_HI * Y_LO
BACK = 3
MESH = pl.DeviceIdType.MESH


def kernel(
    n_gx, n_gy, nodes_ref, w_hbm, src_hbm, out_ref,
    w, src, in_left, in_bottom, out_right, out_top, relay, sig_re, sig_im,
    w_sem, src_sem, send_right, recv_left, send_top, recv_bottom, recv_relay, send_relay,
):
    gx, gy = lax.axis_index("gx"), lax.axis_index("gy")
    step, order = src.shape[2], src.shape[3]
    edge = order // 2
    depth = order // PIECES
    has_left, has_bottom = gx > 0, gy > 0
    has_right, has_top = gx < n_gx - 1, gy < n_gy - 1

    z, y = gx // Y_HI, (gx % Y_HI) * Y_LO + (gy // CORES) % Y_LO

    def on_ring(level, place):
        column = level * Y_HI + place // Y_LO
        row = (gy // (Y_LO * CORES)) * (Y_LO * CORES) + (place % Y_LO) * CORES + gy % CORES
        return column, row

    behind, ahead = (y + RING - BACK) % RING, (y + BACK) % RING
    relay_to = on_ring(z, behind)
    relay_from = on_ring(z, ahead)
    has_relay = relay_from[0] < n_gx - 1
    last_to = on_ring(z + (ahead // Y_LO + 1) // Y_HI, behind)
    origin = gx - 1
    last_from = on_ring(origin // Y_HI, ((origin % Y_HI) * Y_LO + (gy // CORES) % Y_LO + RING - BACK) % RING)

    def load_src(group):
        return pltpu.make_async_copy(
            src_hbm.at[:, pl.ds(group * step, step), :], src.at[group], src_sem.at[group]
        )

    def load_w(half, piece):
        part = (slice(None), pl.ds(piece * depth, depth), pl.ds(half * edge, edge))
        return pltpu.make_async_copy(w_hbm.at[part], w.at[part], w_sem.at[half, piece])

    barrier = pltpu.get_barrier_semaphore()
    for there, device in (
        (has_left, (gx - 1, gy)), (has_bottom, (gx, gy - 1)),
        (has_relay, relay_from), (has_left, last_from),
    ):
        @pl.when(there)
        def _():
            pl.semaphore_signal(barrier, inc=1, device_id=device, device_id_type=MESH)

    for group in range(GROUPS):
        load_src(group).start()
    for half in range(2):
        for piece in range(PIECES):
            load_w(half, piece).start()

    @pl.when(jnp.logical_not(has_left))
    def _():
        in_left[...] = jnp.zeros_like(in_left)

    @pl.when(jnp.logical_not(has_bottom))
    def _():
        in_bottom[...] = jnp.zeros_like(in_bottom)

    block = GROUPS * step // SPANS
    nodes = jnp.concatenate(
        [jnp.full((block, 128), nodes_ref[b].astype(jnp.float32)) for b in range(SPANS)], axis=0
    )
    angles = math.pi * (nodes + 0.5) / SPANS
    sig_re[...] = (0.5 * jnp.cos(angles)).reshape(sig_re.shape)
    sig_im[...] = (0.5 * jnp.sin(angles)).reshape(sig_im.shape)

    def copy_out(out, section, group, dst, send_sem, recv_sem, device):
        return pltpu.make_async_remote_copy(
            src_ref=out.at[section, group], dst_ref=dst,
            send_sem=send_sem.at[section, group], recv_sem=recv_sem,
            device_id=device, device_id_type=MESH,
        )

    def direct(section, group):
        return copy_out(
            out_right, section, group, in_left.at[section, group],
            send_right, recv_left.at[section, group], (gx + 1, gy),
        )

    def first_leg(section, group):
        return copy_out(
            out_right, section, group, relay.at[section],
            send_right, recv_relay.at[section], relay_to,
        )

    def last_leg(section, group):
        return pltpu.make_async_remote_copy(
            src_ref=relay.at[section], dst_ref=in_left.at[section, group],
            send_sem=send_relay.at[section], recv_sem=recv_left.at[section, group],
            device_id=last_to, device_id_type=MESH,
        )

    def upward(section, group):
        return copy_out(
            out_top, section, group, in_bottom.at[section, group],
            send_top, recv_bottom.at[section, group], (gx, gy + 1),
        )

    def turned(section):
        return functools.reduce(jnp.logical_or, [section == other for other in TURNED])

    def first_group(section):
        return sum((section > other).astype(jnp.int32) for other in TURNED) % GROUPS

    def send(side, place, section, group):
        if side == 1:
            upward(section, group).start()
        elif place > 0:
            direct(section, group).start()
        else:
            @pl.when(turned(section))
            def _():
                first_leg(section, group).start()

            @pl.when(jnp.logical_not(turned(section)))
            def _():
                direct(section, group).start()

    def pass_on(section, when):
        @pl.when(jnp.logical_and(has_relay, jnp.logical_and(when, turned(section))))
        def _():
            first_leg(section, 0).wait_recv()
            last_leg(section, first_group(section)).start()

    def product(u, side, first, size):
        half = u.shape[0] // 2
        columns = slice(side * edge, (side + 1) * edge)
        p = jnp.dot(u, w[0, first:first + size, columns], preferred_element_type=jnp.float32)
        q = jnp.dot(u, w[1, first:first + size, columns], preferred_element_type=jnp.float32)
        return p[:half] - q[half:], q[:half] + p[half:]

    def finish(side, section, group, f_re, f_im, real, imag):
        s_re = jnp.concatenate([sig_re[group]] * (edge // 128), axis=1)
        s_im = jnp.concatenate([sig_im[group]] * (edge // 128), axis=1)
        out = out_right if side == 0 else out_top
        out[section, group, 0] = (real + s_re * f_re - s_im * f_im).astype(jnp.bfloat16)
        out[section, group, 1] = (imag + s_re * f_im + s_im * f_re).astype(jnp.bfloat16)

    for group in range(GROUPS):
        load_src(group).wait()
    for side in range(2):
        real, imag = 0.0, 0.0
        columns = slice(side * edge, (side + 1) * edge)
        for piece in range(PIECES):
            load_w(side, piece).wait()
            part = slice(piece * depth, (piece + 1) * depth)
            u = jnp.concatenate(
                [src[group, c, :, part] for c in range(2) for group in range(GROUPS)], axis=0
            )
            more_real, more_imag = product(u, side, 0 + piece * depth, depth)
            real += more_real
            imag += more_imag
        for group in range(GROUPS):
            rows = slice(group * step, (group + 1) * step)
            finish(
                side, 0, group,
                src[group, 0, :, columns].astype(jnp.float32),
                src[group, 1, :, columns].astype(jnp.float32),
                real[rows], imag[rows],
            )
        if side == 0:
            pl.semaphore_wait(
                barrier, 2 * has_right.astype(jnp.int32) + has_top.astype(jnp.int32) + has_relay.astype(jnp.int32)
            )
        for group in range(GROUPS):
            @pl.when(has_right if side == 0 else has_top)
            def _():
                send(side, group, jnp.int32(0), group)

    def section_body(section, _):
        more = section < SECTIONS - 1

        def relay_slot(place, phase):
            if (place, phase) == FIRST_SLOT:
                pass_on(section - 1, section == 1)
            if (place, phase) == RELAY_SLOT:
                pass_on(section, more)
            if (place + GROUPS, phase) == RELAY_SLOT and place + phase > 0:
                pass_on(section - 1, section > 1)

        for place in range(GROUPS):
            group = (first_group(section) + place) % GROUPS
            relay_slot(place, 0)

            def arrived(buffer, columns):
                return [
                    (
                        buffer[section - 1, group, part].astype(jnp.float32)
                        + src[group, part, :, columns].astype(jnp.float32)
                    ).astype(jnp.bfloat16)
                    for part in range(2)
                ]

            @pl.when(has_bottom)
            def _():
                upward(section - 1, group).wait_recv()

            lower = arrived(in_bottom, slice(edge, order))
            u = jnp.concatenate(lower, axis=0)
            partial = [product(u, side, edge, edge) for side in range(2)]
            relay_slot(place, 1)

            @pl.when(has_left)
            def _():
                direct(section - 1, group).wait_recv()

            upper = arrived(in_left, slice(0, edge))
            u = jnp.concatenate(upper, axis=0)
            for side, driven in ((0, upper), (1, lower)):
                real, imag = product(u, side, 0, edge)
                finish(
                    side, section, group,
                    driven[0].astype(jnp.float32), driven[1].astype(jnp.float32),
                    partial[side][0] + real, partial[side][1] + imag,
                )

                @pl.when(jnp.logical_and(has_right if side == 0 else has_top, more))
                def _():
                    send(side, place, section, group)

                if side == 0:
                    relay_slot(place, 2)
        relay_slot(GROUPS, 0)
        return 0

    lax.fori_loop(1, SECTIONS, section_body, 0)

    for group in range(GROUPS):
        rows = pl.ds(group * step, step)
        out_ref[:, rows, :edge] = out_right[SECTIONS - 1, group]
        out_ref[:, rows, edge:] = out_top[SECTIONS - 1, group]

    def drain(section, _):
        for group in range(GROUPS):
            @pl.when(has_right)
            def _():
                direct(section, group).wait_send()

            @pl.when(has_top)
            def _():
                upward(section, group).wait_send()

        @pl.when(jnp.logical_and(has_relay, turned(section)))
        def _():
            last_leg(section, 0).wait_send()
        return 0

    lax.fori_loop(0, SECTIONS - 1, drain, 0)


def solution(mesh):
    n_gx, n_gy = mesh.shape["gx"], mesh.shape["gy"]

    def per_device(transfer, sources, quad_nodes):
        weights, source = transfer[0, 0], sources[0, 0]
        _, rows, order = source.shape
        step, edge = rows // GROUPS, order // 2
        moved = SECTIONS - 1
        dma = pltpu.SemaphoreType.DMA
        vmem = pltpu.VMEM
        outgoing = pl.pallas_call(
            functools.partial(kernel, n_gx, n_gy),
            out_shape=pltpu.VMEM(source.shape, jnp.bfloat16),
            in_specs=[
                pl.BlockSpec(memory_space=pltpu.SMEM),
                pl.BlockSpec(memory_space=pl.ANY),
                pl.BlockSpec(memory_space=pl.ANY),
            ],
            out_specs=pl.BlockSpec(memory_space=pltpu.VMEM),
            scratch_shapes=[
                vmem(weights.shape, jnp.bfloat16),
                vmem((GROUPS, 2, step, order), jnp.bfloat16),
                vmem((moved, GROUPS, 2, step, edge), jnp.bfloat16),
                vmem((moved, GROUPS, 2, step, edge), jnp.bfloat16),
                vmem((SECTIONS, GROUPS, 2, step, edge), jnp.bfloat16),
                vmem((SECTIONS, GROUPS, 2, step, edge), jnp.bfloat16),
                vmem((moved, 2, step, edge), jnp.bfloat16),
                vmem((GROUPS, step, 128), jnp.float32),
                vmem((GROUPS, step, 128), jnp.float32),
                dma((2, PIECES)),
                dma((GROUPS,)),
                dma((moved, GROUPS)),
                dma((moved, GROUPS)),
                dma((moved, GROUPS)),
                dma((moved, GROUPS)),
                dma((moved,)),
                dma((moved,)),
            ],
            compiler_params=pltpu.CompilerParams(
                collective_id=0, has_side_effects=True, vmem_limit_bytes=60 * 1024 * 1024
            ),
        )(quad_nodes, weights, source)
        return outgoing[None, None]

    return jax.shard_map(
        per_device,
        mesh=mesh,
        in_specs=(P("gx", "gy", None, None, None), P("gx", "gy", None, None, None), P()),
        out_specs=P("gx", "gy", None, None, None),
        check_vma=False,
    )
```

```python
import functools
import math

import jax
import jax.numpy as jnp
from jax import lax
from jax.experimental import pallas as pl
from jax.experimental.pallas import tpu as pltpu
from jax.sharding import PartitionSpec as P

SPANS = 8
SECTIONS = 8
GROUPS = 4
PIECES = 4
TURNED = (0, 2, 4, 5)
RELAY_SLOT = (4, 0)
FIRST_SLOT = (0, 2)
Y_HI, Y_LO, CORES = 4, 2, 2
RING = Y_HI * Y_LO
BACK = 3
MESH = pl.DeviceIdType.MESH


def kernel(
    n_gx, n_gy, nodes_ref, w_hbm, src_hbm, out_ref,
    w, src, in_left, in_bottom, out_right, out_top, relay, sig_re, sig_im,
    w_sem, src_sem, send_right, recv_left, send_top, recv_bottom, recv_relay, send_relay,
):
    gx, gy = lax.axis_index("gx"), lax.axis_index("gy")
    step, order = src.shape[2], src.shape[3]
    edge = order // 2
    depth = order // PIECES
    has_left, has_bottom = gx > 0, gy > 0
    has_right, has_top = gx < n_gx - 1, gy < n_gy - 1

    z, y = gx // Y_HI, (gx % Y_HI) * Y_LO + (gy // CORES) % Y_LO

    def on_ring(level, place):
        column = level * Y_HI + place // Y_LO
        row = (gy // (Y_LO * CORES)) * (Y_LO * CORES) + (place % Y_LO) * CORES + gy % CORES
        return column, row

    behind, ahead = (y + RING - BACK) % RING, (y + BACK) % RING
    relay_to = on_ring(z, behind)
    relay_from = on_ring(z, ahead)
    has_relay = relay_from[0] < n_gx - 1
    last_to = on_ring(z + (ahead // Y_LO + 1) // Y_HI, behind)
    origin = gx - 1
    last_from = on_ring(origin // Y_HI, ((origin % Y_HI) * Y_LO + (gy // CORES) % Y_LO + RING - BACK) % RING)

    def load_src(group):
        return pltpu.make_async_copy(
            src_hbm.at[:, pl.ds(group * step, step), :], src.at[group], src_sem.at[group]
        )

    def load_w(half, piece):
        part = (slice(None), pl.ds(piece * depth, depth), pl.ds(half * edge, edge))
        return pltpu.make_async_copy(w_hbm.at[part], w.at[part], w_sem.at[half, piece])

    barrier = pltpu.get_barrier_semaphore()
    for there, device in (
        (has_left, (gx - 1, gy)), (has_bottom, (gx, gy - 1)),
        (has_relay, relay_from), (has_left, last_from),
    ):
        @pl.when(there)
        def _():
            pl.semaphore_signal(barrier, inc=1, device_id=device, device_id_type=MESH)

    for group in range(GROUPS):
        load_src(group).start()
    for half in range(2):
        for piece in range(PIECES):
            load_w(half, piece).start()

    @pl.when(jnp.logical_not(has_left))
    def _():
        in_left[...] = jnp.zeros_like(in_left)

    @pl.when(jnp.logical_not(has_bottom))
    def _():
        in_bottom[...] = jnp.zeros_like(in_bottom)

    block = GROUPS * step // SPANS
    nodes = jnp.concatenate(
        [jnp.full((block, 128), nodes_ref[b].astype(jnp.float32)) for b in range(SPANS)], axis=0
    )
    angles = math.pi * (nodes + 0.5) / SPANS
    sig_re[...] = (0.5 * jnp.cos(angles)).reshape(sig_re.shape)
    sig_im[...] = (0.5 * jnp.sin(angles)).reshape(sig_im.shape)

    def copy_out(out, section, group, dst, send_sem, recv_sem, device):
        return pltpu.make_async_remote_copy(
            src_ref=out.at[section, group], dst_ref=dst,
            send_sem=send_sem.at[section, group], recv_sem=recv_sem,
            device_id=device, device_id_type=MESH,
        )

    def direct(section, group):
        return copy_out(
            out_right, section, group, in_left.at[section, group],
            send_right, recv_left.at[section, group], ((gx + 1) % n_gx, gy),
        )

    def first_leg(section, group):
        return copy_out(
            out_right, section, group, relay.at[section],
            send_right, recv_relay.at[section], relay_to,
        )

    def last_leg(section, group):
        return pltpu.make_async_remote_copy(
            src_ref=relay.at[section], dst_ref=in_left.at[section, group],
            send_sem=send_relay.at[section], recv_sem=recv_left.at[section, group],
            device_id=last_to, device_id_type=MESH,
        )

    def upward(section, group):
        return copy_out(
            out_top, section, group, in_bottom.at[section, group],
            send_top, recv_bottom.at[section, group], (gx, (gy + 1) % n_gy),
        )

    def turned(section):
        return functools.reduce(jnp.logical_or, [section == other for other in TURNED])

    def first_group(section):
        return sum((section > other).astype(jnp.int32) for other in TURNED) % GROUPS

    def send(side, place, section, group):
        if side == 1:
            upward(section, group).start()
        elif place > 0:
            direct(section, group).start()
        else:
            @pl.when(turned(section))
            def _():
                first_leg(section, group).start()

            @pl.when(jnp.logical_not(turned(section)))
            def _():
                direct(section, group).start()

    def pass_on(section, when):
        @pl.when(jnp.logical_and(has_relay, jnp.logical_and(when, turned(section))))
        def _():
            first_leg(section, 0).wait_recv()
            last_leg(section, first_group(section)).start()

    def product(u, side, first, size):
        half = u.shape[0] // 2
        columns = slice(side * edge, (side + 1) * edge)
        p = jnp.dot(u, w[0, first:first + size, columns], preferred_element_type=jnp.float32)
        q = jnp.dot(u, w[1, first:first + size, columns], preferred_element_type=jnp.float32)
        return p[:half] - q[half:], q[:half] + p[half:]

    def finish(side, section, group, f_re, f_im, real, imag):
        s_re = jnp.concatenate([sig_re[group]] * (edge // 128), axis=1)
        s_im = jnp.concatenate([sig_im[group]] * (edge // 128), axis=1)
        out = out_right if side == 0 else out_top
        out[section, group, 0] = (real + s_re * f_re - s_im * f_im).astype(jnp.bfloat16)
        out[section, group, 1] = (imag + s_re * f_im + s_im * f_re).astype(jnp.bfloat16)

    for group in range(GROUPS):
        load_src(group).wait()
    for side in range(2):
        real, imag = 0.0, 0.0
        columns = slice(side * edge, (side + 1) * edge)
        for piece in range(PIECES):
            load_w(side, piece).wait()
            part = slice(piece * depth, (piece + 1) * depth)
            u = jnp.concatenate(
                [src[group, c, :, part] for c in range(2) for group in range(GROUPS)], axis=0
            )
            more_real, more_imag = product(u, side, 0 + piece * depth, depth)
            real += more_real
            imag += more_imag
        for group in range(GROUPS):
            rows = slice(group * step, (group + 1) * step)
            finish(
                side, 0, group,
                src[group, 0, :, columns].astype(jnp.float32),
                src[group, 1, :, columns].astype(jnp.float32),
                real[rows], imag[rows],
            )
        if side == 0:
            pl.semaphore_wait(
                barrier, 2 * has_right.astype(jnp.int32) + has_top.astype(jnp.int32) + has_relay.astype(jnp.int32)
            )
        for group in range(GROUPS):
            @pl.when(has_right if side == 0 else has_top)
            def _():
                send(side, group, jnp.int32(0), group)

    def section_body(section, _):
        more = section < SECTIONS - 1

        def relay_slot(place, phase):
            if (place, phase) == FIRST_SLOT:
                pass_on(section - 1, section == 1)
            if (place, phase) == RELAY_SLOT:
                pass_on(section, more)
            if (place + GROUPS, phase) == RELAY_SLOT and place + phase > 0:
                pass_on(section - 1, section > 1)

        for place in range(GROUPS):
            group = (first_group(section) + place) % GROUPS
            relay_slot(place, 0)

            def arrived(buffer, columns):
                return [
                    (
                        buffer[section - 1, group, part].astype(jnp.float32)
                        + src[group, part, :, columns].astype(jnp.float32)
                    ).astype(jnp.bfloat16)
                    for part in range(2)
                ]

            @pl.when(has_bottom)
            def _():
                upward(section - 1, group).wait_recv()

            lower = arrived(in_bottom, slice(edge, order))
            u = jnp.concatenate(lower, axis=0)
            partial = [product(u, side, edge, edge) for side in range(2)]
            relay_slot(place, 1)

            @pl.when(has_left)
            def _():
                direct(section - 1, group).wait_recv()

            upper = arrived(in_left, slice(0, edge))
            u = jnp.concatenate(upper, axis=0)
            for side, driven in ((0, upper), (1, lower)):
                real, imag = product(u, side, 0, edge)
                finish(
                    side, section, group,
                    driven[0].astype(jnp.float32), driven[1].astype(jnp.float32),
                    partial[side][0] + real, partial[side][1] + imag,
                )

                @pl.when(jnp.logical_and(has_right if side == 0 else has_top, more))
                def _():
                    send(side, place, section, group)

                if side == 0:
                    relay_slot(place, 2)
        relay_slot(GROUPS, 0)
        return 0

    lax.fori_loop(1, SECTIONS, section_body, 0)

    for group in range(GROUPS):
        rows = pl.ds(group * step, step)
        out_ref[:, rows, :edge] = out_right[SECTIONS - 1, group]
        out_ref[:, rows, edge:] = out_top[SECTIONS - 1, group]

    def drain(section, _):
        for group in range(GROUPS):
            @pl.when(has_right)
            def _():
                direct(section, group).wait_send()

            @pl.when(has_top)
            def _():
                upward(section, group).wait_send()

        @pl.when(jnp.logical_and(has_relay, turned(section)))
        def _():
            last_leg(section, 0).wait_send()
        return 0

    lax.fori_loop(0, SECTIONS - 1, drain, 0)


def solution(mesh):
    n_gx, n_gy = mesh.shape["gx"], mesh.shape["gy"]

    def per_device(transfer, sources, quad_nodes):
        weights, source = transfer[0, 0], sources[0, 0]
        _, rows, order = source.shape
        step, edge = rows // GROUPS, order // 2
        moved = SECTIONS - 1
        dma = pltpu.SemaphoreType.DMA
        vmem = pltpu.VMEM
        outgoing = pl.pallas_call(
            functools.partial(kernel, n_gx, n_gy),
            out_shape=pltpu.VMEM(source.shape, jnp.bfloat16),
            in_specs=[
                pl.BlockSpec(memory_space=pltpu.SMEM),
                pl.BlockSpec(memory_space=pl.ANY),
                pl.BlockSpec(memory_space=pl.ANY),
            ],
            out_specs=pl.BlockSpec(memory_space=pltpu.VMEM),
            scratch_shapes=[
                vmem(weights.shape, jnp.bfloat16),
                vmem((GROUPS, 2, step, order), jnp.bfloat16),
                vmem((moved, GROUPS, 2, step, edge), jnp.bfloat16),
                vmem((moved, GROUPS, 2, step, edge), jnp.bfloat16),
                vmem((SECTIONS, GROUPS, 2, step, edge), jnp.bfloat16),
                vmem((SECTIONS, GROUPS, 2, step, edge), jnp.bfloat16),
                vmem((moved, 2, step, edge), jnp.bfloat16),
                vmem((GROUPS, step, 128), jnp.float32),
                vmem((GROUPS, step, 128), jnp.float32),
                dma((2, PIECES)),
                dma((GROUPS,)),
                dma((moved, GROUPS)),
                dma((moved, GROUPS)),
                dma((moved, GROUPS)),
                dma((moved, GROUPS)),
                dma((moved,)),
                dma((moved,)),
            ],
            compiler_params=pltpu.CompilerParams(
                collective_id=0, has_side_effects=True, vmem_limit_bytes=60 * 1024 * 1024
            ),
        )(quad_nodes, weights, source)
        return outgoing[None, None]

    return jax.shard_map(
        per_device,
        mesh=mesh,
        in_specs=(P("gx", "gy", None, None, None), P("gx", "gy", None, None, None), P()),
        out_specs=P("gx", "gy", None, None, None),
        check_vma=False,
    )
```
